32 devices in a mesh: grp: 2 (over y), dp: 16 (over z, x, core).
Axes of the slice: x: 2, y: 2, z: 4, core: 2. Of those that a mesh axis runs over, the one named last changes fastest.
Arguments:
- spectra: bfloat16 [8192, 128], P(('grp', 'dp')), parts along dimension 0, may hold values from -3 to 3
- partners: bfloat16 [8192, 128], P(('grp', 'dp')), parts along dimension 0, may hold values from -3 to 3
- positive: int32 [8192], P(('grp', 'dp')), parts along dimension 0, may hold values from 0 to 4095, each once
Outputs:
- grad_spectra: float32 [8192, 128], P(('grp', 'dp')), parts along dimension 0
- grad_partners: float32 [8192, 128], P(('grp', 'dp')), parts along dimension 0
The draws below stay inside these ranges and needn't reach their ends.
There are 2 independent parts, one for each index of `grp`. The reference program is written for one: setup_inputs(seed, part) draws one part's arguments, and reference() takes and returns one part's arrays. A program takes and returns all parts, laid end to end along the dimension named above; each array names one. Nothing has to cross between parts.
All inputs are finite; a program needn't handle non-finite values.
Results may differ from the reference program's by a relative error of at most 0.0017.
Values may be sent and summed in bfloat16 or wider, within the bound.
A program may use at most 128 MiB of HBM per device.

```python
import math
import jax
import jax.numpy as jnp
from jax import lax

EMBED = 128
ROWS = 4096


def signs_table(key):
    flips = jax.random.bernoulli(key, 0.5, (ROWS // 128, EMBED))
    return jnp.where(flips, 1.0, -1.0).astype(jnp.float32)


def group_lift(group):
    return 1.2 + 0.9 * (group % 3).astype(jnp.float32)


def draw_spectra(key, part):
    table = signs_table(key)
    key = jax.random.fold_in(key, 5)
    first_key, second_key = jax.random.split(key, 2)
    base = 0.25 * jax.random.normal(first_key, (ROWS, EMBED), jnp.float32)
    scales = jnp.exp(jax.random.uniform(second_key, (ROWS, 1), jnp.float32, math.log(0.5), math.log(5.0)))
    values = jnp.clip(scales * base, -3.0, 3.0)
    index = jnp.arange(ROWS, dtype=jnp.int32)
    group = index // 128
    planted = group_lift(group)[:, None] * table[group]
    values = jnp.where((index % 128 == 0)[:, None], planted, values)
    return values.astype(jnp.bfloat16)


def draw_partners(key, part):
    table = signs_table(key)
    key = jax.random.fold_in(key, 9)
    first_key, second_key = jax.random.split(key, 2)
    base = 0.25 * jax.random.normal(first_key, (ROWS, EMBED), jnp.float32)
    scales = jnp.exp(jax.random.uniform(second_key, (ROWS, 1), jnp.float32, math.log(0.5), math.log(5.0)))
    values = jnp.clip(scales * base, -3.0, 3.0)
    index = jnp.arange(ROWS, dtype=jnp.int32)
    group = index // 128
    offset = index % 128
    twin = 3.0 * table[group]
    lift = group_lift(group)
    column = jnp.arange(EMBED, dtype=jnp.int32)
    near_first = (3.0 - 2.0 / lift)[:, None] * table[group]
    near = jnp.where((column == 0)[None, :], near_first, twin)
    values = jnp.where((offset == 50)[:, None], twin, values)
    values = jnp.where((offset == 100)[:, None], near, values)
    return values.astype(jnp.bfloat16)


def setup_inputs(seed: int = 0, part: int = 0) -> dict:
    arg_keys = jax.random.split(jax.random.key(seed), 4)
    own_keys = jax.random.split(jax.random.fold_in(arg_keys[3], part), 4)
    return {
        "spectra": draw_spectra(jax.random.fold_in(jax.random.fold_in(arg_keys[3], part), 71), part),
        "partners": draw_partners(jax.random.fold_in(jax.random.fold_in(arg_keys[3], part), 71), part),
        "positive": jax.random.permutation(own_keys[2], ROWS).astype(jnp.int32),
    }


def reference(spectra, partners, positive):
    block = math.gcd(ROWS, 1024)
    count = ROWS // block
    spec_blocks = spectra.reshape(count, block, EMBED)
    pos_blocks = positive.reshape(count, block)
    columns = jnp.arange(ROWS, dtype=jnp.int32)

    def scores(rows):
        return jnp.dot(rows, partners.T, preferred_element_type=jnp.float32)

    def first(carry, rows):
        peak_now, total_now = carry
        logits = scores(rows)
        peak = jnp.max(logits, axis=1)
        lse = peak + jnp.log(jnp.sum(jnp.exp(logits - peak[:, None]), axis=1))
        new_peak = jnp.maximum(peak_now, jnp.max(logits, axis=0))
        total = total_now * jnp.exp(peak_now - new_peak) + jnp.sum(jnp.exp(logits - new_peak[None, :]), axis=0)
        return (new_peak, total), lse

    start_peak = jnp.full((ROWS,), -jnp.inf, dtype=jnp.float32)
    start_total = jnp.zeros((ROWS,), jnp.float32)
    (col_peak, col_total), row_lse = lax.scan(first, (start_peak, start_total), spec_blocks)
    col_lse = col_peak + jnp.log(col_total)

    def third(carry, items):
        rows, lse, pos = items
        logits = scores(rows)
        target = (pos[:, None] == columns[None, :]).astype(jnp.float32)
        weights = (jnp.exp(logits - lse[:, None]) + jnp.exp(logits - col_lse[None, :]) - 2.0 * target).astype(jnp.bfloat16)
        grad_rows = jnp.dot(weights, partners, preferred_element_type=jnp.float32)
        carry = carry + jnp.dot(weights.T, rows, preferred_element_type=jnp.float32)
        return carry, grad_rows

    grad_partners, grad_blocks = lax.scan(third, jnp.zeros((ROWS, EMBED), jnp.float32), (spec_blocks, row_lse, pos_blocks))
    return grad_blocks.reshape(ROWS, EMBED), grad_partners
```

```python
import functools
import math

import jax
import jax.numpy as jnp
from jax import lax
from jax.experimental import pallas as pl
from jax.experimental.pallas import tpu as pltpu
from jax.sharding import PartitionSpec as P

LOG2E = math.log2(math.e)
TILE = 256


def kernel(
    n_p, n_z, s_ref, p_ref, pos_ref, gs_ref, gp_ref,
    s_all, s_t, p_all, pos_all, pos_col, scores, lane_max, lane_sum, row_col, col_lse,
    row_stat, col_stat, gs_acc, gp_part, gs_recv, gp_recv,
    s_send, s_recv, i_send, i_recv, p_send, p_recv,
    rs_send, rs_recv, cs_send, cs_recv, gs_send, gs_rsem, gp_send, gp_rsem,
):
    rows, embed = s_ref.shape
    block_rows = n_p * rows
    tile = min(TILE, rows)
    me = lax.axis_index("dp")
    my_z, my_q = me // n_p, me % n_p

    def plane(k):
        q = lax.rem(my_q + k, n_p)
        return q, my_z * n_p + q

    def column(k):
        z = lax.rem(my_z + k, n_z)
        return z, z * n_p + my_q

    def copy(src, dst, send, recv, device):
        return pltpu.make_async_remote_copy(
            src_ref=src, dst_ref=dst, send_sem=send, recv_sem=recv,
            device_id={"dp": device}, device_id_type=pl.DeviceIdType.MESH,
        )

    def each(count, body):
        if count <= 4:
            for k in range(1, count):
                body(k)
        else:
            def step(k, carry):
                body(k)
                return carry
            lax.fori_loop(1, count, step, 0)

    def s_copy(k, slot, device):
        return copy(s_ref, s_all.at[slot], s_send.at[k], s_recv.at[slot], device)

    def i_copy(k, slot, device):
        return copy(pos_ref, pos_all.at[slot], i_send.at[k], i_recv.at[slot], device)

    def p_copy(k, slot, device):
        return copy(p_ref, p_all.at[slot], p_send.at[k], p_recv.at[slot], device)

    def rs_copy(k, slot, device):
        return copy(row_stat.at[my_q], row_stat.at[slot], rs_send.at[k], rs_recv.at[slot], device)

    def cs_copy(k, slot, device):
        return copy(col_stat.at[my_z], col_stat.at[slot], cs_send.at[k], cs_recv.at[slot], device)

    def gs_copy(k, q, slot, device):
        return copy(gs_acc.at[q], gs_recv.at[slot], gs_send.at[k], gs_rsem.at[slot], device)

    def gp_copy(k, z, slot, device):
        return copy(gp_part.at[z], gp_recv.at[slot], gp_send.at[k], gp_rsem.at[slot], device)

    barrier = pltpu.get_barrier_semaphore()

    def greet(device):
        pl.semaphore_signal(
            barrier, inc=1, device_id={"dp": device}, device_id_type=pl.DeviceIdType.MESH
        )

    each(n_p, lambda k: greet(plane(k)[1]))
    each(n_z, lambda k: greet(column(k)[1]))
    pl.semaphore_wait(barrier, n_p + n_z - 2)

    each(n_p, lambda k: s_copy(k, my_q, plane(k)[1]).start())
    each(n_z, lambda k: p_copy(k, my_z, column(k)[1]).start())
    each(n_p, lambda k: i_copy(k, my_q, plane(k)[1]).start())

    s_all[my_q] = s_ref[...]
    p_all[my_z] = p_ref[...]
    pos_all[my_q] = pos_ref[...]

    def arrived(k):
        q, device = plane(k)
        s_copy(k, q, device).wait_recv()

    each(n_p, arrived)

    def first(k, start):
        z, device = column(k)
        if not start:
            p_copy(k, z, device).wait_recv()
        part = p_all[z]
        col_max = None
        for q in range(n_p):
            for t in range(rows // tile):
                sub = pl.ds(t * tile, tile)
                block = lax.dot_general(
                    s_all[q, sub, :], part, (((1,), (1,)), ((), ())),
                    preferred_element_type=jnp.float32,
                ) * LOG2E
                scores[z, q, sub, :] = block
                here = jnp.max(block, axis=0, keepdims=True)
                col_max = here if col_max is None else jnp.maximum(col_max, here)
        col_sum = jnp.zeros((1, rows), jnp.float32)
        for q in range(n_p):
            for t in range(rows // tile):
                sub = pl.ds(t * tile, tile)
                block = scores[z, q, sub, :]
                col_sum += jnp.sum(jnp.exp2(block - col_max), axis=0, keepdims=True)
                pieces = [block[:, g * 128:(g + 1) * 128] for g in range(rows // 128)]
                peak = functools.reduce(jnp.maximum, pieces)
                if not start:
                    old = lane_max[q, sub, :]
                    peak = jnp.maximum(peak, old)
                total = sum(jnp.exp2(piece - peak) for piece in pieces)
                if not start:
                    total += lane_sum[q, sub, :] * jnp.exp2(old - peak)
                lane_max[q, sub, :] = peak
                lane_sum[q, sub, :] = total
        col_stat[my_z, z, 0:1, :] = col_max
        col_stat[my_z, z, 1:2, :] = col_sum

    first(0, True)
    each(n_z, lambda k: first(k, False))

    each(n_z, lambda k: cs_copy(k, my_z, column(k)[1]).start())
    for q in range(n_p):
        peaks = lane_max[q].T
        peak = jnp.max(peaks, axis=0, keepdims=True)
        row_stat[my_q, q, 0:1, :] = peak
        row_stat[my_q, q, 1:2, :] = jnp.sum(
            lane_sum[q].T * jnp.exp2(peaks - peak), axis=0, keepdims=True
        )
    each(n_p, lambda k: rs_copy(k, my_q, plane(k)[1]).start())

    def pos_arrived(k):
        q, device = plane(k)
        i_copy(k, q, device).wait_recv()

    each(n_p, pos_arrived)
    for q in range(n_p):
        s_t[q] = s_all[q].T
        spread = jnp.broadcast_to(pos_all[q].astype(jnp.float32), (128, rows))
        pos_col[q] = spread.T.astype(jnp.int32)

    def rs_arrived(k):
        q, device = plane(k)
        rs_copy(k, q, device).wait_recv()

    def cs_arrived(k):
        z, device = column(k)
        cs_copy(k, z, device).wait_recv()

    each(n_p, rs_arrived)
    for q in range(n_p):
        stat = row_stat[:, q]
        peak = jnp.max(stat[:, 0, :], axis=0, keepdims=True)
        total = jnp.sum(stat[:, 1, :] * jnp.exp2(stat[:, 0, :] - peak), axis=0, keepdims=True)
        lse = peak + jnp.log(total) * LOG2E
        row_col[q] = jnp.broadcast_to(lse, (128, rows)).T
    each(n_z, cs_arrived)
    for z in range(n_z):
        stat = col_stat[:, z]
        peak = jnp.max(stat[:, 0, :], axis=0, keepdims=True)
        total = jnp.sum(stat[:, 1, :] * jnp.exp2(stat[:, 0, :] - peak), axis=0, keepdims=True)
        col_lse[z] = peak + jnp.log(total) * LOG2E

    def second(k, start, last):
        z, device = column(k)
        part = p_all[z]
        lse = col_lse[z]
        first_col = (z * n_p + my_q) * rows
        out = None
        for q in range(n_p):
            for t in range(rows // tile):
                sub = pl.ds(t * tile, tile)
                shift = row_col[q, sub, :]
                target = pos_col[q, sub, :] - first_col
                lane = lax.broadcasted_iota(jnp.int32, (tile, 128), 1)
                pieces = []
                for g in range(rows // 128):
                    cut = slice(g * 128, (g + 1) * 128)
                    block = scores[z, q, sub, cut]
                    value = jnp.exp2(block - shift) + jnp.exp2(block - lse[:, cut])
                    value = value - jnp.where(target == lane + g * 128, 2.0, 0.0)
                    pieces.append(value.astype(jnp.bfloat16))
                weights = jnp.concatenate(pieces, axis=1)
                grad = jnp.dot(weights, part, preferred_element_type=jnp.float32)
                if not start:
                    grad += gs_acc[q, sub, :]
                gs_acc[q, sub, :] = grad
                term = jnp.dot(s_t[q, :, sub], weights, preferred_element_type=jnp.float32)
                out = term if out is None else out + term
        gp_part[z] = out
        if not last:
            gp_copy(k, z, my_z, device).start()

    if n_z > 1:
        second(1, True, False)
        if n_z <= 4:
            for k in range(2, n_z):
                second(k, False, False)
        else:
            def step(k, carry):
                second(k, False, False)
                return carry
            lax.fori_loop(2, n_z, step, 0)
    second(0, n_z == 1, True)

    def gs_start(k):
        q, device = plane(k)
        gs_copy(k, q, my_q, device).start()

    each(n_p, gs_start)

    gs_ref[...] = gs_acc[my_q]
    gp_recv[my_z] = gp_part[my_z]

    def gs_add(k):
        q, device = plane(k)
        gs_copy(k, q, q, device).wait_recv()
        gs_ref[...] += gs_recv[q]

    each(n_p, gs_add)

    def gp_add(k):
        z, device = column(k)
        gp_copy(k, z, z, device).wait_recv()
        gp_recv[my_z] += gp_recv[z]

    each(n_z, gp_add)
    gp_ref[...] = gp_recv[my_z].T

    def sent_plane(k):
        q, device = plane(k)
        s_copy(k, q, device).wait_send()
        i_copy(k, q, device).wait_send()
        rs_copy(k, q, device).wait_send()
        gs_copy(k, q, q, device).wait_send()

    def sent_column(k):
        z, device = column(k)
        p_copy(k, z, device).wait_send()
        cs_copy(k, z, device).wait_send()
        gp_copy(k, z, z, device).wait_send()

    each(n_p, sent_plane)
    each(n_z, sent_column)


def solution(mesh):
    ranks = mesh.shape["dp"]
    n_p = 1 << (int(math.log2(ranks)) // 2)
    n_z = ranks // n_p

    def shards(spectra, partners, positive):
        rows, embed = spectra.shape
        f32, bf16 = jnp.float32, jnp.bfloat16
        vmem, dma = pltpu.VMEM, pltpu.SemaphoreType.DMA
        elements = n_p * n_z * rows * rows
        return pl.pallas_call(
            functools.partial(kernel, n_p, n_z),
            out_shape=[jax.ShapeDtypeStruct((rows, embed), f32)] * 2,
            in_specs=[pl.BlockSpec(memory_space=pltpu.VMEM)] * 3,
            out_specs=[pl.BlockSpec(memory_space=pltpu.VMEM)] * 2,
            scratch_shapes=[
                vmem((n_p, rows, embed), bf16),
                vmem((n_p, embed, rows), bf16),
                vmem((n_z, rows, embed), bf16),
                vmem((n_p, 1, rows), jnp.int32),
                vmem((n_p, rows, 128), jnp.int32),
                vmem((n_z, n_p, rows, rows), f32),
                vmem((n_p, rows, 128), f32),
                vmem((n_p, rows, 128), f32),
                vmem((n_p, rows, 128), f32),
                vmem((n_z, 1, rows), f32),
                vmem((n_p, n_p, 2, rows), f32),
                vmem((n_z, n_z, 2, rows), f32),
                vmem((n_p, rows, embed), f32),
                vmem((n_z, embed, rows), f32),
                vmem((n_p, rows, embed), f32),
                vmem((n_z, embed, rows), f32),
            ] + [dma((n_p,))] * 4 + [dma((n_z,))] * 2
            + [dma((n_p,))] * 2 + [dma((n_z,))] * 2 + [dma((n_p,))] * 2 + [dma((n_z,))] * 2,
            compiler_params=pltpu.CompilerParams(
                collective_id=0, has_side_effects=True, vmem_limit_bytes=56 * 1024 * 1024
            ),
            cost_estimate=pl.CostEstimate(
                flops=6 * elements * embed, transcendentals=4 * elements,
                bytes_accessed=8 * rows * embed * (n_p + n_z),
            ),
        )(spectra, partners, positive.reshape(1, rows))

    placed = (P(("grp", "dp"), None), P(("grp", "dp"), None), P(("grp", "dp")))
    return jax.shard_map(
        shards,
        mesh=mesh,
        in_specs=placed,
        out_specs=(P(("grp", "dp"), None), P(("grp", "dp"), None)),
        check_vma=False,
    )
```

```python
import functools
import math

import jax
import jax.numpy as jnp
from jax import lax
from jax.experimental import pallas as pl
from jax.experimental.pallas import tpu as pltpu
from jax.sharding import PartitionSpec as P

LOG2E = math.log2(math.e)
TILE = 256
VMEM_BYTES = 60 << 20


def kernel(
    n_p, n_z, s_ref, p_ref, pos_ref, gs_ref, gp_ref,
    s_all, s_t, p_all, pos_all, pos_col, scores, lane_max, lane_sum, row_col, col_lse,
    row_stat, col_stat, gs_acc, gp_sum, gs_out, gp_out, gs_code, gp_code, gs_got, gp_got,
    gs_step, gp_step, gs_step_got, gp_step_got,
    s_send, s_recv, i_send, i_recv, p_send, p_recv,
    rs_send, rs_recv, cs_send, cs_recv, gs_send, gs_recv, gp_send, gp_recv,
    gt_send, gt_recv, pt_send, pt_recv, local,
):
    rows, embed = s_ref.shape
    block_rows = n_p * rows
    tile = min(TILE, rows)
    me = lax.axis_index("dp")
    my_z, my_q = me // n_p, me % n_p

    def plane(k):
        q = lax.rem(my_q + k, n_p)
        return q, my_z * n_p + q

    def column(k):
        z = lax.rem(my_z + k, n_z)
        return z, z * n_p + my_q

    def copy(src, dst, send, recv, device):
        return pltpu.make_async_remote_copy(
            src_ref=src, dst_ref=dst, send_sem=send, recv_sem=recv,
            device_id={"dp": device}, device_id_type=pl.DeviceIdType.MESH,
        )

    def each(count, body):
        if count <= 4:
            for k in range(1, count):
                body(k)
        else:
            def step(k, carry):
                body(k)
                return carry
            lax.fori_loop(1, count, step, 0)

    def s_copy(k, slot, device):
        return copy(s_all.at[my_q], s_all.at[slot], s_send.at[k], s_recv.at[slot], device)

    def i_copy(k, slot, device):
        return copy(pos_all.at[my_q], pos_all.at[slot], i_send.at[k], i_recv.at[slot], device)

    def p_copy(k, slot, device):
        return copy(p_all.at[my_z], p_all.at[slot], p_send.at[k], p_recv.at[slot], device)

    def rs_copy(k, slot, device):
        return copy(row_stat.at[my_q], row_stat.at[slot], rs_send.at[k], rs_recv.at[slot], device)

    def cs_copy(k, slot, device):
        return copy(col_stat.at[my_z], col_stat.at[slot], cs_send.at[k], cs_recv.at[slot], device)

    def gs_copies(k, q, slot, device):
        return (
            copy(gs_code.at[q], gs_got.at[slot], gs_send.at[k], gs_recv.at[slot], device),
            copy(gs_step.at[q], gs_step_got.at[slot], gt_send.at[k], gt_recv.at[slot], device),
        )

    def gp_copies(k, z, slot, device):
        return (
            copy(gp_code.at[z], gp_got.at[slot], gp_send.at[k], gp_recv.at[slot], device),
            copy(gp_step.at[z], gp_step_got.at[slot], pt_send.at[k], pt_recv.at[slot], device),
        )

    own = (
        pltpu.make_async_copy(s_ref, s_all.at[my_q], local.at[0]),
        pltpu.make_async_copy(p_ref, p_all.at[my_z], local.at[1]),
        pltpu.make_async_copy(pos_ref, pos_all.at[my_q], local.at[2]),
    )
    for item in own:
        item.start()

    barrier = pltpu.get_barrier_semaphore()

    def greet(device):
        pl.semaphore_signal(
            barrier, inc=1, device_id={"dp": device}, device_id_type=pl.DeviceIdType.MESH
        )

    each(n_p, lambda k: greet(plane(k)[1]))
    each(n_z, lambda k: greet(column(k)[1]))
    for item in own:
        item.wait()
    pl.semaphore_wait(barrier, n_p + n_z - 2)

    each(n_p, lambda k: s_copy(k, my_q, plane(k)[1]).start())
    each(n_z, lambda k: p_copy(k, my_z, column(k)[1]).start())
    each(n_p, lambda k: i_copy(k, my_q, plane(k)[1]).start())

    def arrived(k):
        q, device = plane(k)
        s_copy(k, q, device).wait_recv()

    each(n_p, arrived)

    def first(k, start):
        z, device = column(k)
        if not start:
            p_copy(k, z, device).wait_recv()
        part = p_all[z]
        col_max = None
        for q in range(n_p):
            for t in range(rows // tile):
                sub = pl.ds(t * tile, tile)
                block = lax.dot_general(
                    s_all[q, sub, :], part, (((1,), (1,)), ((), ())),
                    preferred_element_type=jnp.float32,
                ) * LOG2E
                scores[z, q, sub, :] = block
                here = jnp.max(block, axis=0, keepdims=True)
                col_max = here if col_max is None else jnp.maximum(col_max, here)
        col_sum = jnp.zeros((1, rows), jnp.float32)
        for q in range(n_p):
            for t in range(rows // tile):
                sub = pl.ds(t * tile, tile)
                block = scores[z, q, sub, :]
                col_sum += jnp.sum(jnp.exp2(block - col_max), axis=0, keepdims=True)
                pieces = [block[:, g * 128:(g + 1) * 128] for g in range(rows // 128)]
                peak = functools.reduce(jnp.maximum, pieces)
                if not start:
                    old = lane_max[q, sub, :]
                    peak = jnp.maximum(peak, old)
                total = sum(jnp.exp2(piece - peak) for piece in pieces)
                if not start:
                    total += lane_sum[q, sub, :] * jnp.exp2(old - peak)
                lane_max[q, sub, :] = peak
                lane_sum[q, sub, :] = total
        col_stat[my_z, z, 0:1, :] = col_max
        col_stat[my_z, z, 1:2, :] = col_sum

    first(0, True)
    def pos_arrived(k):
        q, device = plane(k)
        i_copy(k, q, device).wait_recv()

    each(n_p, pos_arrived)
    for q in range(n_p):
        s_t[q] = s_all[q].T
        spread = jnp.broadcast_to(pos_all[q].astype(jnp.float32), (128, rows))
        pos_col[q] = spread.T.astype(jnp.int32)

    each(n_z, lambda k: first(k, False))

    each(n_z, lambda k: cs_copy(k, my_z, column(k)[1]).start())
    for q in range(n_p):
        peaks = lane_max[q].T
        peak = jnp.max(peaks, axis=0, keepdims=True)
        row_stat[my_q, q, 0:1, :] = peak
        row_stat[my_q, q, 1:2, :] = jnp.sum(
            lane_sum[q].T * jnp.exp2(peaks - peak), axis=0, keepdims=True
        )
    each(n_p, lambda k: rs_copy(k, my_q, plane(k)[1]).start())

    def rs_arrived(k):
        q, device = plane(k)
        rs_copy(k, q, device).wait_recv()

    def cs_arrived(k):
        z, device = column(k)
        cs_copy(k, z, device).wait_recv()

    each(n_p, rs_arrived)
    for q in range(n_p):
        stat = row_stat[:, q]
        peak = jnp.max(stat[:, 0, :], axis=0, keepdims=True)
        total = jnp.sum(stat[:, 1, :] * jnp.exp2(stat[:, 0, :] - peak), axis=0, keepdims=True)
        lse = peak + jnp.log(total) * LOG2E
        row_col[q] = jnp.broadcast_to(lse, (128, rows)).T
    each(n_z, cs_arrived)
    for z in range(n_z):
        stat = col_stat[:, z]
        peak = jnp.max(stat[:, 0, :], axis=0, keepdims=True)
        total = jnp.sum(stat[:, 1, :] * jnp.exp2(stat[:, 0, :] - peak), axis=0, keepdims=True)
        col_lse[z] = peak + jnp.log(total) * LOG2E

    def encode(values):
        peak = jnp.maximum(jnp.max(jnp.abs(values), axis=0, keepdims=True), 1e-30)
        code = jnp.floor(values * (32767.0 / peak) + 0.5).astype(jnp.int32).astype(jnp.int16)
        return code, peak * (1.0 / 32767.0)

    def decode(code, step):
        return code.astype(jnp.int32).astype(jnp.float32) * step

    def second(k, start, last):
        z, device = column(k)
        part = p_all[z]
        lse = col_lse[z]
        first_col = (z * n_p + my_q) * rows
        out = None
        for q in range(n_p):
            for t in range(rows // tile):
                sub = pl.ds(t * tile, tile)
                shift = row_col[q, sub, :]
                target = pos_col[q, sub, :] - first_col
                lane = lax.broadcasted_iota(jnp.int32, (tile, 128), 1)
                pieces = []
                for g in range(rows // 128):
                    cut = slice(g * 128, (g + 1) * 128)
                    block = scores[z, q, sub, cut]
                    value = jnp.exp2(block - shift) + jnp.exp2(block - lse[:, cut])
                    value = value - jnp.where(target == lane + g * 128, 2.0, 0.0)
                    pieces.append(value.astype(jnp.bfloat16))
                weights = jnp.concatenate(pieces, axis=1)
                grad = jnp.dot(weights, part, preferred_element_type=jnp.float32)
                if not start:
                    grad += gs_acc[q, sub, :]
                gs_acc[q, sub, :] = grad
                term = jnp.dot(s_t[q, :, sub], weights, preferred_element_type=jnp.float32)
                out = term if out is None else out + term
        if last:
            gp_sum[...] = out
        else:
            gp_code[z], gp_step[z] = encode(out)
            for item in gp_copies(k, z, my_z, device):
                item.start()

    if n_z > 1:
        second(1, True, False)
        if n_z <= 4:
            for k in range(2, n_z):
                second(k, False, False)
        else:
            def step(k, carry):
                second(k, False, False)
                return carry
            lax.fori_loop(2, n_z, step, 0)
    second(0, n_z == 1, True)

    def gs_start(k):
        q, device = plane(k)
        gs_code[q], gs_step[q] = encode(gs_acc[q])
        for item in gs_copies(k, q, my_q, device):
            item.start()

    each(n_p, gs_start)

    gs_out[...] = gs_acc[my_q]

    def gs_add(k):
        q, device = plane(k)
        for item in gs_copies(k, q, q, device):
            item.wait_recv()
        gs_out[...] += decode(gs_got[q], gs_step_got[q])

    each(n_p, gs_add)
    gs_done = pltpu.make_async_copy(gs_out, gs_ref, local.at[0])
    gs_done.start()

    def gp_add(k):
        z, device = column(k)
        for item in gp_copies(k, z, z, device):
            item.wait_recv()
        gp_sum[...] += decode(gp_got[z], gp_step_got[z])

    each(n_z, gp_add)
    gp_out[...] = gp_sum[...].T
    gp_done = pltpu.make_async_copy(gp_out, gp_ref, local.at[1])
    gp_done.start()

    def sent_plane(k):
        q, device = plane(k)
        s_copy(k, q, device).wait_send()
        i_copy(k, q, device).wait_send()
        rs_copy(k, q, device).wait_send()
        for item in gs_copies(k, q, q, device):
            item.wait_send()

    def sent_column(k):
        z, device = column(k)
        p_copy(k, z, device).wait_send()
        cs_copy(k, z, device).wait_send()
        for item in gp_copies(k, z, z, device):
            item.wait_send()

    each(n_p, sent_plane)
    each(n_z, sent_column)
    gs_done.wait()
    gp_done.wait()


def finish(gs_in, gp_in, gs_ref, gp_ref):
    gs_ref[...] = gs_in[...]
    gp_ref[...] = gp_in[...]


def solution(mesh):
    ranks = mesh.shape["dp"]
    n_p = 1 << (int(math.log2(ranks)) // 2)
    n_z = ranks // n_p

    def shards(spectra, partners, positive):
        rows, embed = spectra.shape
        f32, bf16, i32 = jnp.float32, jnp.bfloat16, jnp.int32
        vmem, dma = pltpu.VMEM, pltpu.SemaphoreType.DMA
        elements = n_p * n_z * rows * rows
        shapes = [
            ((n_p, rows, embed), bf16),
            ((n_p, embed, rows), bf16),
            ((n_z, rows, embed), bf16),
            ((n_p, 1, rows), i32),
            ((n_p, rows, 128), i32),
            ((n_z, n_p, rows, rows), f32),
            ((n_p, rows, 128), f32),
            ((n_p, rows, 128), f32),
            ((n_p, rows, 128), f32),
            ((n_z, 1, rows), f32),
            ((n_p, n_p, 2, rows), f32),
            ((n_z, n_z, 2, rows), f32),
            ((n_p, rows, embed), f32),
            ((embed, rows), f32),
            ((rows, embed), f32),
            ((rows, embed), f32),
            ((n_p, rows, embed), jnp.int16),
            ((n_z, embed, rows), jnp.int16),
            ((n_p, rows, embed), jnp.int16),
            ((n_z, embed, rows), jnp.int16),
            ((n_p, 1, embed), f32),
            ((n_z, 1, rows), f32),
            ((n_p, 1, embed), f32),
            ((n_z, 1, rows), f32),
        ]
        outputs = [jax.ShapeDtypeStruct((rows, embed), f32)] * 2
        grads = pl.pallas_call(
            functools.partial(kernel, n_p, n_z),
            out_shape=outputs,
            in_specs=[pl.BlockSpec(memory_space=pltpu.HBM)] * 3,
            out_specs=[pl.BlockSpec(memory_space=pl.ANY)] * 2,
            scratch_shapes=[vmem(shape, kind) for shape, kind in shapes]
            + [dma((n_p,))] * 4 + [dma((n_z,))] * 2
            + [dma((n_p,))] * 2 + [dma((n_z,))] * 2 + [dma((n_p,))] * 2 + [dma((n_z,))] * 2
            + [dma((n_p,))] * 2 + [dma((n_z,))] * 2 + [dma((3,))],
            compiler_params=pltpu.CompilerParams(
                collective_id=0, has_side_effects=True, vmem_limit_bytes=VMEM_BYTES
            ),
            cost_estimate=pl.CostEstimate(
                flops=6 * elements * embed, transcendentals=4 * elements,
                bytes_accessed=8 * rows * embed * (n_p + n_z),
            ),
        )(spectra, partners, positive.reshape(1, rows))
        return pl.pallas_call(
            finish,
            out_shape=outputs,
            in_specs=[pl.BlockSpec(memory_space=pltpu.VMEM)] * 2,
            out_specs=[pl.BlockSpec(memory_space=pltpu.VMEM)] * 2,
            compiler_params=pltpu.CompilerParams(vmem_limit_bytes=VMEM_BYTES),
        )(*grads)

    placed = (P(("grp", "dp"), None), P(("grp", "dp"), None), P(("grp", "dp")))
    return jax.shard_map(
        shards,
        mesh=mesh,
        in_specs=placed,
        out_specs=(P(("grp", "dp"), None), P(("grp", "dp"), None)),
        check_vma=False,
    )
```

```python
import functools
import math

import jax
import jax.numpy as jnp
from jax import lax
from jax.experimental import pallas as pl
from jax.experimental.pallas import tpu as pltpu
from jax.sharding import PartitionSpec as P

LOG2E = math.log2(math.e)
TILE = 256
VMEM_BYTES = 60 << 20


def kernel(
    n_p, n_z, s_ref, p_ref, pos_ref,
    gs_own, gp_own, gs_got, gp_got, gs_step_got, gp_step_got,
    s_all, s_t, p_all, pos_all, pos_col, scores, row_col, col_lse,
    row_stat, col_stat, gs_acc, gp_sum, gs_code, gp_code, gs_step, gp_step,
    s_send, s_recv, i_send, i_recv, p_send, p_recv,
    rs_send, rs_recv, cs_send, cs_recv, gs_send, gs_recv, gp_send, gp_recv,
    gt_send, gt_recv, pt_send, pt_recv, local,
):
    rows, embed = s_ref.shape
    block_rows = n_p * rows
    tile = min(TILE, rows)
    me = lax.axis_index("dp")
    my_z, my_q = me // n_p, me % n_p

    def plane(k):
        q = lax.rem(my_q + k, n_p)
        return q, my_z * n_p + q

    def column(k):
        z = lax.rem(my_z + k, n_z)
        return z, z * n_p + my_q

    def ascending(k):
        z = k - 1 + (k - 1 - my_z + n_z) // n_z
        return z, z * n_p + my_q

    upper = 2 * my_z // n_z

    def farthest(k):
        return ascending(upper * k + (1 - upper) * (n_z - k))

    def nearest(k):
        return farthest(n_z - k)

    def place(sender, owner):
        return sender - (sender - owner - 1 + n_z) // n_z

    def copy(src, dst, send, recv, device):
        return pltpu.make_async_remote_copy(
            src_ref=src, dst_ref=dst, send_sem=send, recv_sem=recv,
            device_id={"dp": device}, device_id_type=pl.DeviceIdType.MESH,
        )

    def each(count, body):
        if count <= 4:
            for k in range(1, count):
                body(k)
        else:
            def step(k, carry):
                body(k)
                return carry
            lax.fori_loop(1, count, step, 0)

    def s_copy(k, slot, device):
        return copy(s_all.at[my_q], s_all.at[slot], s_send.at[k], s_recv.at[slot], device)

    def i_copy(k, slot, device):
        return copy(pos_all.at[my_q], pos_all.at[slot], i_send.at[k], i_recv.at[slot], device)

    def p_copy(k, slot, device):
        return copy(p_all.at[my_z], p_all.at[slot], p_send.at[k], p_recv.at[slot], device)

    def rs_copy(k, slot, device):
        return copy(row_stat.at[my_q], row_stat.at[slot], rs_send.at[k], rs_recv.at[slot], device)

    def cs_copy(k, slot, device):
        return copy(col_stat.at[my_z], col_stat.at[slot], cs_send.at[k], cs_recv.at[slot], device)

    def gs_copies(k, q, device):
        at = k - 1
        return (
            copy(gs_code.at[q], gs_got.at[at], gs_send.at[at], gs_recv.at[at], device),
            copy(gs_step.at[q], gs_step_got.at[at], gt_send.at[at], gt_recv.at[at], device),
        )

    def gp_copies(k, z, at, device):
        return (
            copy(gp_code.at[z], gp_got.at[at], gp_send.at[k - 1], gp_recv.at[at], device),
            copy(gp_step.at[z], gp_step_got.at[at], pt_send.at[k - 1], pt_recv.at[at], device),
        )

    own = (
        pltpu.make_async_copy(s_ref, s_all.at[my_q], local.at[0]),
        pltpu.make_async_copy(p_ref, p_all.at[my_z], local.at[1]),
        pltpu.make_async_copy(pos_ref, pos_all.at[my_q], local.at[2]),
    )
    for item in own:
        item.start()

    barrier = pltpu.get_barrier_semaphore()

    def greet(device):
        pl.semaphore_signal(
            barrier, inc=1, device_id={"dp": device}, device_id_type=pl.DeviceIdType.MESH
        )

    each(n_p, lambda k: greet(plane(k)[1]))
    each(n_z, lambda k: greet(column(k)[1]))
    for item in own:
        item.wait()
    pl.semaphore_wait(barrier, n_p + n_z - 2)

    each(n_z, lambda k: p_copy(k, my_z, nearest(k)[1]).start())
    each(n_p, lambda k: s_copy(k, my_q, plane(k)[1]).start())
    each(n_p, lambda k: i_copy(k, my_q, plane(k)[1]).start())

    def arrived(k):
        q, device = plane(k)
        s_copy(k, q, device).wait_recv()

    each(n_p, arrived)

    def first(k, start, last):
        z, device = (my_z, me) if start else nearest(k)
        if not start:
            p_copy(k, z, device).wait_recv()
        part = p_all[z]
        col_max = None
        for q in range(n_p):
            for t in range(rows // tile):
                sub = pl.ds(t * tile, tile)
                block = lax.dot_general(
                    s_all[q, sub, :], part, (((1,), (1,)), ((), ())),
                    preferred_element_type=jnp.float32,
                ) * LOG2E
                scores[z, q, sub, :] = block
                here = jnp.max(block, axis=0, keepdims=True)
                col_max = here if col_max is None else jnp.maximum(col_max, here)
        col_sum = jnp.zeros((1, rows), jnp.float32)
        for q in range(n_p):
            for t in range(rows // tile):
                block = scores[z, q, pl.ds(t * tile, tile), :]
                col_sum += jnp.sum(jnp.exp2(block - col_max), axis=0, keepdims=True)
        col_stat[my_z, z, 0:1, :] = col_max
        col_stat[my_z, z, 1:2, :] = col_sum
        if last:
            each(n_z, lambda k: cs_copy(k, my_z, column(k)[1]).start())
        for q in range(n_p):
            block = lax.dot_general(
                part, s_all[q], (((1,), (1,)), ((), ())), preferred_element_type=jnp.float32
            ) * LOG2E
            peak = jnp.max(block, axis=0, keepdims=True)
            if not start:
                old = row_stat[my_q, q, 0:1, :]
                peak = jnp.maximum(peak, old)
            total = jnp.sum(jnp.exp2(block - peak), axis=0, keepdims=True)
            if not start:
                total += row_stat[my_q, q, 1:2, :] * jnp.exp2(old - peak)
            row_stat[my_q, q, 0:1, :] = peak
            row_stat[my_q, q, 1:2, :] = total

    first(0, True, n_z == 1)
    def pos_arrived(k):
        q, device = plane(k)
        i_copy(k, q, device).wait_recv()

    each(n_p, pos_arrived)
    for q in range(n_p):
        s_t[q] = s_all[q].T
        spread = jnp.broadcast_to(pos_all[q].astype(jnp.float32), (128, rows))
        pos_col[q] = spread.T.astype(jnp.int32)

    each(n_z - 1, lambda k: first(k, False, False))
    if n_z > 1:
        first(n_z - 1, False, True)

    each(n_p, lambda k: rs_copy(k, my_q, plane(k)[1]).start())

    def rs_arrived(k):
        q, device = plane(k)
        rs_copy(k, q, device).wait_recv()

    def cs_arrived(k):
        z, device = column(k)
        cs_copy(k, z, device).wait_recv()

    each(n_p, rs_arrived)
    for q in range(n_p):
        stat = row_stat[:, q]
        peak = jnp.max(stat[:, 0, :], axis=0, keepdims=True)
        total = jnp.sum(stat[:, 1, :] * jnp.exp2(stat[:, 0, :] - peak), axis=0, keepdims=True)
        lse = peak + jnp.log(total) * LOG2E
        row_col[q] = jnp.broadcast_to(lse, (128, rows)).T
    each(n_z, cs_arrived)
    for z in range(n_z):
        stat = col_stat[:, z]
        peak = jnp.max(stat[:, 0, :], axis=0, keepdims=True)
        total = jnp.sum(stat[:, 1, :] * jnp.exp2(stat[:, 0, :] - peak), axis=0, keepdims=True)
        col_lse[z] = peak + jnp.log(total) * LOG2E

    def encode(values):
        peak = jnp.maximum(jnp.max(jnp.abs(values), axis=0, keepdims=True), 1e-30)
        code = jnp.floor(values * (32767.0 / peak) + 0.5).astype(jnp.int32).astype(jnp.int16)
        return code, peak * (1.0 / 32767.0)

    def second(k, start, last):
        z, device = (my_z, me) if last else farthest(k)
        part = p_all[z]
        lse = col_lse[z]
        first_col = (z * n_p + my_q) * rows
        out = None
        for q in range(n_p):
            for t in range(rows // tile):
                sub = pl.ds(t * tile, tile)
                shift = row_col[q, sub, :]
                target = pos_col[q, sub, :] - first_col
                lane = lax.broadcasted_iota(jnp.int32, (tile, 128), 1)
                pieces = []
                for g in range(rows // 128):
                    cut = slice(g * 128, (g + 1) * 128)
                    block = scores[z, q, sub, cut]
                    value = jnp.exp2(block - shift) + jnp.exp2(block - lse[:, cut])
                    value = value - jnp.where(target == lane + g * 128, 2.0, 0.0)
                    pieces.append(value.astype(jnp.bfloat16))
                weights = jnp.concatenate(pieces, axis=1)
                grad = jnp.dot(weights, part, preferred_element_type=jnp.float32)
                if not start:
                    grad += gs_acc[q, sub, :]
                gs_acc[q, sub, :] = grad
                term = jnp.dot(s_t[q, :, sub], weights, preferred_element_type=jnp.float32)
                out = term if out is None else out + term
        if last:
            gp_sum[...] = out
        else:
            gp_code[z], gp_step[z] = encode(out)
            for item in gp_copies(k, z, place(my_z, z), device):
                item.start()

    if n_z > 1:
        second(1, True, False)
        if n_z <= 4:
            for k in range(2, n_z):
                second(k, False, False)
        else:
            def step(k, carry):
                second(k, False, False)
                return carry
            lax.fori_loop(2, n_z, step, 0)
    second(0, n_z == 1, True)

    def gs_start(k):
        q, device = plane(k)
        gs_code[q], gs_step[q] = encode(gs_acc[q])
        for item in gs_copies(k, q, device):
            item.start()

    each(n_p, gs_start)

    kept = (
        pltpu.make_async_copy(gs_acc.at[my_q], gs_own, local.at[0]),
        pltpu.make_async_copy(gp_sum, gp_own, local.at[1]),
    )
    for item in kept:
        item.start()

    def sent_plane(k):
        q, device = plane(k)
        s_copy(k, q, device).wait_send()
        i_copy(k, q, device).wait_send()
        rs_copy(k, q, device).wait_send()
        for item in gs_copies(k, q, device):
            item.wait()

    def sent_column(k):
        z, device = column(k)
        p_copy(k, z, device).wait_send()
        cs_copy(k, z, device).wait_send()
        for item in gp_copies(k, z, k - 1, device):
            item.wait()

    each(n_p, sent_plane)
    each(n_z, sent_column)
    for item in kept:
        item.wait()


def finish(gs_own, gp_own, gs_got, gp_got, gs_step, gp_step, gs_ref, gp_ref):
    def total(own, codes, steps):
        value = own[...]
        for k in range(codes.shape[0]):
            value += codes[k].astype(jnp.int32).astype(jnp.float32) * steps[k]
        return value

    gs_ref[...] = total(gs_own, gs_got, gs_step)
    gp_ref[...] = total(gp_own, gp_got, gp_step).T


def solution(mesh):
    ranks = mesh.shape["dp"]
    n_p = 1 << (int(math.log2(ranks)) // 2)
    n_z = ranks // n_p

    def shards(spectra, partners, positive):
        rows, embed = spectra.shape
        f32, bf16, i32, i16 = jnp.float32, jnp.bfloat16, jnp.int32, jnp.int16
        vmem, dma = pltpu.VMEM, pltpu.SemaphoreType.DMA
        elements = n_p * n_z * rows * rows
        shapes = [
            ((n_p, rows, embed), bf16),
            ((n_p, embed, rows), bf16),
            ((n_z, rows, embed), bf16),
            ((n_p, 1, rows), i32),
            ((n_p, rows, 128), i32),
            ((n_z, n_p, rows, rows), f32),
            ((n_p, rows, 128), f32),
            ((n_z, 1, rows), f32),
            ((n_p, n_p, 2, rows), f32),
            ((n_z, n_z, 2, rows), f32),
            ((n_p, rows, embed), f32),
            ((embed, rows), f32),
            ((n_p, rows, embed), i16),
            ((n_z, embed, rows), i16),
            ((n_p, 1, embed), f32),
            ((n_z, 1, rows), f32),
        ]
        outputs = [jax.ShapeDtypeStruct((rows, embed), f32)] * 2
        parts = [
            ((rows, embed), f32),
            ((embed, rows), f32),
            ((n_p - 1, rows, embed), i16),
            ((n_z - 1, embed, rows), i16),
            ((n_p - 1, 1, embed), f32),
            ((n_z - 1, 1, rows), f32),
        ]
        grads = pl.pallas_call(
            functools.partial(kernel, n_p, n_z),
            out_shape=[jax.ShapeDtypeStruct(shape, kind) for shape, kind in parts],
            in_specs=[pl.BlockSpec(memory_space=pltpu.HBM)] * 3,
            out_specs=[pl.BlockSpec(memory_space=pl.ANY)] * len(parts),
            scratch_shapes=[vmem(shape, kind) for shape, kind in shapes]
            + [dma((n_p,))] * 4 + [dma((n_z,))] * 2
            + [dma((n_p,))] * 2 + [dma((n_z,))] * 2 + [dma((n_p,))] * 2 + [dma((n_z,))] * 2
            + [dma((n_p,))] * 2 + [dma((n_z,))] * 2 + [dma((3,))],
            compiler_params=pltpu.CompilerParams(
                collective_id=0, has_side_effects=True, vmem_limit_bytes=VMEM_BYTES
            ),
            cost_estimate=pl.CostEstimate(
                flops=6 * elements * embed, transcendentals=4 * elements,
                bytes_accessed=8 * rows * embed * (n_p + n_z),
            ),
        )(spectra, partners, positive.reshape(1, rows))
        return pl.pallas_call(
            finish,
            out_shape=outputs,
            in_specs=[pl.BlockSpec(memory_space=pltpu.VMEM)] * len(parts),
            out_specs=[pl.BlockSpec(memory_space=pltpu.VMEM)] * 2,
            compiler_params=pltpu.CompilerParams(vmem_limit_bytes=VMEM_BYTES),
        )(*grads)

    placed = (P(("grp", "dp"), None), P(("grp", "dp"), None), P(("grp", "dp")))
    return jax.shard_map(
        shards,
        mesh=mesh,
        in_specs=placed,
        out_specs=(P(("grp", "dp"), None), P(("grp", "dp"), None)),
        check_vma=False,
    )
```

```python
import functools
import math

import jax
import jax.numpy as jnp
from jax import lax
from jax.experimental import pallas as pl
from jax.experimental.pallas import tpu as pltpu
from jax.sharding import PartitionSpec as P

LOG2E = math.log2(math.e)
TILE = 256
VMEM_BYTES = 60 << 20


def kernel(
    n_p, n_z, s_ref, p_ref, pos_ref,
    gs_own, gp_own, gs_got, gp_got, gs_step_got, gp_step_got,
    s_all, s_t, p_all, pos_all, pos_col, scores, row_col, col_lse,
    row_run, row_stat, col_stat, gs_acc, gp_sum, gs_code, gp_code, gs_step, gp_step,
    s_send, s_recv, i_send, i_recv, p_send, p_recv,
    rs_send, rs_recv, cs_send, cs_recv, gs_send, gs_recv, gp_send, gp_recv,
    gt_send, gt_recv, pt_send, pt_recv, local,
):
    rows, embed = s_ref.shape
    block_rows = n_p * rows
    tile = min(TILE, rows)
    me = lax.axis_index("dp")
    my_z, my_q = me // n_p, me % n_p

    def plane(k):
        q = lax.rem(my_q + k, n_p)
        return q, my_z * n_p + q

    def column(k):
        z = lax.rem(my_z + k, n_z)
        return z, z * n_p + my_q

    def ascending(k):
        z = k - 1 + (k - 1 - my_z + n_z) // n_z
        return z, z * n_p + my_q

    upper = 2 * my_z // n_z

    def farthest(k):
        return ascending(upper * k + (1 - upper) * (n_z - k))

    def nearest(k):
        return farthest(n_z - k)

    def place(sender, owner):
        return sender - (sender - owner - 1 + n_z) // n_z

    def copy(src, dst, send, recv, device):
        return pltpu.make_async_remote_copy(
            src_ref=src, dst_ref=dst, send_sem=send, recv_sem=recv,
            device_id={"dp": device}, device_id_type=pl.DeviceIdType.MESH,
        )

    def each(count, body):
        if count <= 4:
            for k in range(1, count):
                body(k)
        else:
            def step(k, carry):
                body(k)
                return carry
            lax.fori_loop(1, count, step, 0)

    def s_copy(k, slot, device):
        return copy(s_all.at[my_q], s_all.at[slot], s_send.at[k], s_recv.at[slot], device)

    def i_copy(k, slot, device):
        return copy(pos_all.at[my_q], pos_all.at[slot], i_send.at[k], i_recv.at[slot], device)

    def p_copy(k, slot, device):
        return copy(p_all.at[my_z], p_all.at[slot], p_send.at[k], p_recv.at[slot], device)

    def rs_copy(k, slot, device):
        return copy(row_stat.at[my_q], row_stat.at[slot], rs_send.at[k], rs_recv.at[slot], device)

    def cs_copy(k, slot, device):
        return copy(col_stat.at[my_z], col_stat.at[slot], cs_send.at[k], cs_recv.at[slot], device)

    def gs_copies(k, q, device):
        at = k - 1
        return (
            copy(gs_code.at[q], gs_got.at[at], gs_send.at[at], gs_recv.at[at], device),
            copy(gs_step.at[q], gs_step_got.at[at], gt_send.at[at], gt_recv.at[at], device),
        )

    def gp_copies(k, z, at, device):
        return (
            copy(gp_code.at[z], gp_got.at[at], gp_send.at[k - 1], gp_recv.at[at], device),
            copy(gp_step.at[z], gp_step_got.at[at], pt_send.at[k - 1], pt_recv.at[at], device),
        )

    own = (
        pltpu.make_async_copy(s_ref, s_all.at[my_q], local.at[0]),
        pltpu.make_async_copy(p_ref, p_all.at[my_z], local.at[1]),
        pltpu.make_async_copy(pos_ref, pos_all.at[my_q], local.at[2]),
    )
    for item in own:
        item.start()

    barrier = pltpu.get_barrier_semaphore()

    def greet(device):
        pl.semaphore_signal(
            barrier, inc=1, device_id={"dp": device}, device_id_type=pl.DeviceIdType.MESH
        )

    each(n_p, lambda k: greet(plane(k)[1]))
    each(n_z, lambda k: greet(column(k)[1]))
    for item in own:
        item.wait()
    pl.semaphore_wait(barrier, n_p + n_z - 2)

    each(n_z, lambda k: p_copy(k, my_z, nearest(k)[1]).start())
    each(n_p, lambda k: s_copy(k, my_q, plane(k)[1]).start())
    each(n_p, lambda k: i_copy(k, my_q, plane(k)[1]).start())

    def arrived(k):
        q, device = plane(k)
        s_copy(k, q, device).wait_recv()

    each(n_p, arrived)

    def first(k, start, last):
        z, device = (my_z, me) if start else nearest(k)
        if not start:
            p_copy(k, z, device).wait_recv()
        part = p_all[z]
        col_max = None
        for q in range(n_p):
            for t in range(rows // tile):
                sub = pl.ds(t * tile, tile)
                block = lax.dot_general(
                    s_all[q, sub, :], part, (((1,), (1,)), ((), ())),
                    preferred_element_type=jnp.float32,
                ) * LOG2E
                scores[z, q, sub, :] = block
                here = jnp.max(block, axis=0, keepdims=True)
                col_max = here if col_max is None else jnp.maximum(col_max, here)
        col_sum = jnp.zeros((1, rows), jnp.float32)
        for q in range(n_p):
            for t in range(rows // tile):
                block = scores[z, q, pl.ds(t * tile, tile), :]
                col_sum += jnp.sum(jnp.exp2(block - col_max), axis=0, keepdims=True)
        col_stat[my_z, z] = col_max + jnp.log(col_sum) * LOG2E
        if last:
            each(n_z, lambda k: cs_copy(k, my_z, column(k)[1]).start())
        for q in range(n_p):
            block = lax.dot_general(
                part, s_all[q], (((1,), (1,)), ((), ())), preferred_element_type=jnp.float32
            ) * LOG2E
            peak = jnp.max(block, axis=0, keepdims=True)
            if not start:
                old = row_run[q, 0:1, :]
                peak = jnp.maximum(peak, old)
            total = jnp.sum(jnp.exp2(block - peak), axis=0, keepdims=True)
            if not start:
                total += row_run[q, 1:2, :] * jnp.exp2(old - peak)
            if last:
                row_stat[my_q, q] = peak + jnp.log(total) * LOG2E
            else:
                row_run[q, 0:1, :] = peak
                row_run[q, 1:2, :] = total

    first(0, True, n_z == 1)
    def pos_arrived(k):
        q, device = plane(k)
        i_copy(k, q, device).wait_recv()

    each(n_p, pos_arrived)
    for q in range(n_p):
        s_t[q] = s_all[q].T
        spread = jnp.broadcast_to(pos_all[q].astype(jnp.float32), (128, rows))
        pos_col[q] = spread.T.astype(jnp.int32)

    each(n_z - 1, lambda k: first(k, False, False))
    if n_z > 1:
        first(n_z - 1, False, True)

    each(n_p, lambda k: rs_copy(k, my_q, plane(k)[1]).start())

    def rs_arrived(k):
        q, device = plane(k)
        rs_copy(k, q, device).wait_recv()

    def cs_arrived(k):
        z, device = column(k)
        cs_copy(k, z, device).wait_recv()

    each(n_p, rs_arrived)
    for q in range(n_p):
        stat = row_stat[:, q]
        peak = jnp.max(stat, axis=0)
        total = jnp.sum(jnp.exp2(stat - peak), axis=0)
        lse = peak + jnp.log(total) * LOG2E
        row_col[q] = jnp.broadcast_to(lse, (128, rows)).T
    each(n_z, cs_arrived)
    for z in range(n_z):
        stat = col_stat[:, z]
        peak = jnp.max(stat, axis=0)
        total = jnp.sum(jnp.exp2(stat - peak), axis=0)
        col_lse[z] = peak + jnp.log(total) * LOG2E

    def encode(values):
        peak = jnp.maximum(jnp.max(jnp.abs(values), axis=0, keepdims=True), 1e-30)
        code = jnp.floor(values * (32767.0 / peak) + 0.5).astype(jnp.int32).astype(jnp.int16)
        return code, peak * (1.0 / 32767.0)

    def second(k, start, last):
        z, device = (my_z, me) if last else farthest(k)
        part = p_all[z]
        lse = col_lse[z]
        first_col = (z * n_p + my_q) * rows
        out = None
        for q in range(n_p):
            for t in range(rows // tile):
                sub = pl.ds(t * tile, tile)
                shift = row_col[q, sub, :]
                target = pos_col[q, sub, :] - first_col
                lane = lax.broadcasted_iota(jnp.int32, (tile, 128), 1)
                pieces = []
                for g in range(rows // 128):
                    cut = slice(g * 128, (g + 1) * 128)
                    block = scores[z, q, sub, cut]
                    value = jnp.exp2(block - shift) + jnp.exp2(block - lse[:, cut])
                    value = value - jnp.where(target == lane + g * 128, 2.0, 0.0)
                    pieces.append(value.astype(jnp.bfloat16))
                weights = jnp.concatenate(pieces, axis=1)
                grad = jnp.dot(weights, part, preferred_element_type=jnp.float32)
                if not start:
                    grad += gs_acc[q, sub, :]
                gs_acc[q, sub, :] = grad
                term = jnp.dot(s_t[q, :, sub], weights, preferred_element_type=jnp.float32)
                out = term if out is None else out + term
        if last:
            gp_sum[...] = out
        else:
            gp_code[z], gp_step[z] = encode(out)
            for item in gp_copies(k, z, place(my_z, z), device):
                item.start()

    if n_z > 1:
        second(1, True, False)
        if n_z <= 4:
            for k in range(2, n_z):
                second(k, False, False)
        else:
            def step(k, carry):
                second(k, False, False)
                return carry
            lax.fori_loop(2, n_z, step, 0)
    second(0, n_z == 1, True)

    def gs_start(k):
        q, device = plane(k)
        gs_code[q], gs_step[q] = encode(gs_acc[q])
        for item in gs_copies(k, q, device):
            item.start()

    each(n_p, gs_start)

    kept = (
        pltpu.make_async_copy(gs_acc.at[my_q], gs_own, local.at[0]),
        pltpu.make_async_copy(gp_sum, gp_own, local.at[1]),
    )
    for item in kept:
        item.start()

    def sent_plane(k):
        q, device = plane(k)
        s_copy(k, q, device).wait_send()
        i_copy(k, q, device).wait_send()
        rs_copy(k, q, device).wait_send()
        for item in gs_copies(k, q, device):
            item.wait()

    def sent_column(k):
        z, device = column(k)
        p_copy(k, z, device).wait_send()
        cs_copy(k, z, device).wait_send()
        for item in gp_copies(k, z, k - 1, device):
            item.wait()

    each(n_p, sent_plane)
    each(n_z, sent_column)
    for item in kept:
        item.wait()


def finish(gs_own, gp_own, gs_got, gp_got, gs_step, gp_step, gs_ref, gp_ref):
    def total(own, codes, steps):
        value = own[...]
        for k in range(codes.shape[0]):
            value += codes[k].astype(jnp.int32).astype(jnp.float32) * steps[k]
        return value

    gs_ref[...] = total(gs_own, gs_got, gs_step)
    gp_ref[...] = total(gp_own, gp_got, gp_step).T


def solution(mesh):
    ranks = mesh.shape["dp"]
    n_p = 1 << (int(math.log2(ranks)) // 2)
    n_z = ranks // n_p

    def shards(spectra, partners, positive):
        rows, embed = spectra.shape
        f32, bf16, i32, i16 = jnp.float32, jnp.bfloat16, jnp.int32, jnp.int16
        vmem, dma = pltpu.VMEM, pltpu.SemaphoreType.DMA
        elements = n_p * n_z * rows * rows
        shapes = [
            ((n_p, rows, embed), bf16),
            ((n_p, embed, rows), bf16),
            ((n_z, rows, embed), bf16),
            ((n_p, 1, rows), i32),
            ((n_p, rows, 128), i32),
            ((n_z, n_p, rows, rows), f32),
            ((n_p, rows, 128), f32),
            ((n_z, 1, rows), f32),
            ((n_p, 2, rows), f32),
            ((n_p, n_p, 1, rows), f32),
            ((n_z, n_z, 1, rows), f32),
            ((n_p, rows, embed), f32),
            ((embed, rows), f32),
            ((n_p, rows, embed), i16),
            ((n_z, embed, rows), i16),
            ((n_p, 1, embed), f32),
            ((n_z, 1, rows), f32),
        ]
        outputs = [jax.ShapeDtypeStruct((rows, embed), f32)] * 2
        parts = [
            ((rows, embed), f32),
            ((embed, rows), f32),
            ((n_p - 1, rows, embed), i16),
            ((n_z - 1, embed, rows), i16),
            ((n_p - 1, 1, embed), f32),
            ((n_z - 1, 1, rows), f32),
        ]
        grads = pl.pallas_call(
            functools.partial(kernel, n_p, n_z),
            out_shape=[jax.ShapeDtypeStruct(shape, kind) for shape, kind in parts],
            in_specs=[pl.BlockSpec(memory_space=pltpu.HBM)] * 3,
            out_specs=[pl.BlockSpec(memory_space=pl.ANY)] * len(parts),
            scratch_shapes=[vmem(shape, kind) for shape, kind in shapes]
            + [dma((n_p,))] * 4 + [dma((n_z,))] * 2
            + [dma((n_p,))] * 2 + [dma((n_z,))] * 2 + [dma((n_p,))] * 2 + [dma((n_z,))] * 2
            + [dma((n_p,))] * 2 + [dma((n_z,))] * 2 + [dma((3,))],
            compiler_params=pltpu.CompilerParams(
                collective_id=0, has_side_effects=True, vmem_limit_bytes=VMEM_BYTES
            ),
            cost_estimate=pl.CostEstimate(
                flops=6 * elements * embed, transcendentals=4 * elements,
                bytes_accessed=8 * rows * embed * (n_p + n_z),
            ),
        )(spectra, partners, positive.reshape(1, rows))
        return pl.pallas_call(
            finish,
            out_shape=outputs,
            in_specs=[pl.BlockSpec(memory_space=pltpu.VMEM)] * len(parts),
            out_specs=[pl.BlockSpec(memory_space=pltpu.VMEM)] * 2,
            compiler_params=pltpu.CompilerParams(vmem_limit_bytes=VMEM_BYTES),
        )(*grads)

    placed = (P(("grp", "dp"), None), P(("grp", "dp"), None), P(("grp", "dp")))
    return jax.shard_map(
        shards,
        mesh=mesh,
        in_specs=placed,
        out_specs=(P(("grp", "dp"), None), P(("grp", "dp"), None)),
        check_vma=False,
    )
```

```python
import functools
import math

import jax
import jax.numpy as jnp
from jax import lax
from jax.experimental import pallas as pl
from jax.experimental.pallas import tpu as pltpu
from jax.sharding import PartitionSpec as P

LOG2E = math.log2(math.e)
TILE = 256
VMEM_BYTES = 60 << 20


def kernel(
    n_p, n_z, s_ref, p_ref, pos_ref,
    gs_own, gp_own, gs_got, gp_got, gs_step_got, gp_step_got,
    s_all, s_t, p_all, pos_all, pos_col, scores, row_col, col_lse,
    row_run, row_stat, col_stat, gs_acc, gp_sum, gs_code, gp_code, gs_step, gp_step,
    s_send, s_recv, i_send, i_recv, p_send, p_recv,
    rs_send, rs_recv, cs_send, cs_recv, gs_send, gs_recv, gp_send, gp_recv,
    gt_send, gt_recv, pt_send, pt_recv, local,
):
    rows, embed = s_ref.shape
    block_rows = n_p * rows
    tile = min(TILE, rows)
    me = lax.axis_index("dp")
    my_z, my_q = me // n_p, me % n_p

    def plane(k):
        q = lax.rem(my_q + k, n_p)
        return q, my_z * n_p + q

    def column(k):
        z = lax.rem(my_z + k, n_z)
        return z, z * n_p + my_q

    def ascending(k):
        z = k - 1 + (k - 1 - my_z + n_z) // n_z
        return z, z * n_p + my_q

    upper = 2 * my_z // n_z

    def farthest(k):
        return ascending(upper * k + (1 - upper) * (n_z - k))

    def nearest(k):
        return farthest(n_z - k)

    def place(sender, owner):
        return sender - (sender - owner - 1 + n_z) // n_z

    def copy(src, dst, send, recv, device):
        return pltpu.make_async_remote_copy(
            src_ref=src, dst_ref=dst, send_sem=send, recv_sem=recv,
            device_id={"dp": device}, device_id_type=pl.DeviceIdType.MESH,
        )

    def each(count, body):
        if count <= 4:
            for k in range(1, count):
                body(k)
        else:
            def step(k, carry):
                body(k)
                return carry
            lax.fori_loop(1, count, step, 0)

    def s_copy(k, slot, device):
        return copy(s_all.at[my_q], s_all.at[slot], s_send.at[k], s_recv.at[slot], device)

    def i_copy(k, slot, device):
        return copy(pos_all.at[my_q], pos_all.at[slot], i_send.at[k], i_recv.at[slot], device)

    def p_copy(k, slot, device):
        return copy(p_all.at[my_z], p_all.at[slot], p_send.at[k], p_recv.at[slot], device)

    def rs_copy(k, slot, device):
        return copy(row_stat.at[my_q], row_stat.at[slot], rs_send.at[k], rs_recv.at[slot], device)

    def cs_copy(k, slot, device):
        return copy(col_stat.at[my_z], col_stat.at[slot], cs_send.at[k], cs_recv.at[slot], device)

    def gs_copies(k, q, device):
        at = k - 1
        return (
            copy(gs_code.at[q], gs_got.at[at], gs_send.at[at], gs_recv.at[at], device),
            copy(gs_step.at[q], gs_step_got.at[at], gt_send.at[at], gt_recv.at[at], device),
        )

    def gp_copies(k, z, at, device):
        return (
            copy(gp_code.at[z], gp_got.at[at], gp_send.at[k - 1], gp_recv.at[at], device),
            copy(gp_step.at[z], gp_step_got.at[at], pt_send.at[k - 1], pt_recv.at[at], device),
        )

    own = (
        pltpu.make_async_copy(s_ref, s_all.at[my_q], local.at[0]),
        pltpu.make_async_copy(p_ref, p_all.at[my_z], local.at[1]),
        pltpu.make_async_copy(pos_ref, pos_all.at[my_q], local.at[2]),
    )
    barrier = pltpu.get_barrier_semaphore()

    def greet(device):
        pl.semaphore_signal(
            barrier, inc=1, device_id={"dp": device}, device_id_type=pl.DeviceIdType.MESH
        )

    each(n_z, lambda k: greet(farthest(k)[1]))
    each(n_p, lambda k: greet(plane(k)[1]))
    for item in own:
        item.start()
    for item in own:
        item.wait()
    pl.semaphore_wait(barrier, n_p + n_z - 2)

    each(n_z, lambda k: p_copy(k, my_z, nearest(k)[1]).start())
    each(n_p, lambda k: s_copy(k, my_q, plane(k)[1]).start())
    each(n_p, lambda k: i_copy(k, my_q, plane(k)[1]).start())

    def arrived(k):
        q, device = plane(k)
        s_copy(k, q, device).wait_recv()

    each(n_p, arrived)

    def first(k, start, last):
        z, device = (my_z, me) if start else nearest(k)
        if not start:
            p_copy(k, z, device).wait_recv()
        part = p_all[z]
        col_max = None
        for q in range(n_p):
            for t in range(rows // tile):
                sub = pl.ds(t * tile, tile)
                block = lax.dot_general(
                    s_all[q, sub, :], part, (((1,), (1,)), ((), ())),
                    preferred_element_type=jnp.float32,
                ) * LOG2E
                scores[z, q, sub, :] = block
                here = jnp.max(block, axis=0, keepdims=True)
                col_max = here if col_max is None else jnp.maximum(col_max, here)
        col_sum = jnp.zeros((1, rows), jnp.float32)
        for q in range(n_p):
            for t in range(rows // tile):
                block = scores[z, q, pl.ds(t * tile, tile), :]
                col_sum += jnp.sum(jnp.exp2(block - col_max), axis=0, keepdims=True)
        col_stat[my_z, z] = col_max + jnp.log(col_sum) * LOG2E
        if last:
            each(n_z, lambda k: cs_copy(k, my_z, column(k)[1]).start())
        for q in range(n_p):
            block = lax.dot_general(
                part, s_all[q], (((1,), (1,)), ((), ())), preferred_element_type=jnp.float32
            ) * LOG2E
            peak = jnp.max(block, axis=0, keepdims=True)
            if not start:
                old = row_run[q, 0:1, :]
                peak = jnp.maximum(peak, old)
            total = jnp.sum(jnp.exp2(block - peak), axis=0, keepdims=True)
            if not start:
                total += row_run[q, 1:2, :] * jnp.exp2(old - peak)
            if last:
                row_stat[my_q, q] = peak + jnp.log(total) * LOG2E
            else:
                row_run[q, 0:1, :] = peak
                row_run[q, 1:2, :] = total

    first(0, True, n_z == 1)
    def pos_arrived(k):
        q, device = plane(k)
        i_copy(k, q, device).wait_recv()

    each(n_p, pos_arrived)
    for q in range(n_p):
        s_t[q] = s_all[q].T
        spread = jnp.broadcast_to(pos_all[q].astype(jnp.float32), (128, rows))
        pos_col[q] = spread.T.astype(jnp.int32)

    each(n_z - 1, lambda k: first(k, False, False))
    if n_z > 1:
        first(n_z - 1, False, True)

    each(n_p, lambda k: rs_copy(k, my_q, plane(k)[1]).start())

    def rs_arrived(k):
        q, device = plane(k)
        rs_copy(k, q, device).wait_recv()

    def cs_arrived(k):
        z, device = column(k)
        cs_copy(k, z, device).wait_recv()

    each(n_p, rs_arrived)
    for q in range(n_p):
        stat = row_stat[:, q]
        peak = jnp.max(stat, axis=0)
        total = jnp.sum(jnp.exp2(stat - peak), axis=0)
        lse = peak + jnp.log(total) * LOG2E
        row_col[q] = jnp.broadcast_to(lse, (128, rows)).T
    each(n_z, cs_arrived)
    for z in range(n_z):
        stat = col_stat[:, z]
        peak = jnp.max(stat, axis=0)
        total = jnp.sum(jnp.exp2(stat - peak), axis=0)
        col_lse[z] = peak + jnp.log(total) * LOG2E

    def encode(values):
        peak = jnp.maximum(jnp.max(jnp.abs(values), axis=0, keepdims=True), 1e-30)
        code = jnp.floor(values * (32767.0 / peak) + 0.5).astype(jnp.int32).astype(jnp.int16)
        return code, peak * (1.0 / 32767.0)

    def second(k, start, last):
        z, device = (my_z, me) if last else farthest(k)
        part = p_all[z]
        lse = col_lse[z]
        first_col = (z * n_p + my_q) * rows
        out = None
        for q in range(n_p):
            for t in range(rows // tile):
                sub = pl.ds(t * tile, tile)
                shift = row_col[q, sub, :]
                target = pos_col[q, sub, :] - first_col
                lane = lax.broadcasted_iota(jnp.int32, (tile, 128), 1)
                pieces = []
                for g in range(rows // 128):
                    cut = slice(g * 128, (g + 1) * 128)
                    block = scores[z, q, sub, cut]
                    value = jnp.exp2(block - shift) + jnp.exp2(block - lse[:, cut])
                    value = value - jnp.where(target == lane + g * 128, 2.0, 0.0)
                    pieces.append(value.astype(jnp.bfloat16))
                weights = jnp.concatenate(pieces, axis=1)
                grad = jnp.dot(weights, part, preferred_element_type=jnp.float32)
                if not start:
                    grad += gs_acc[q, sub, :]
                gs_acc[q, sub, :] = grad
                term = jnp.dot(s_t[q, :, sub], weights, preferred_element_type=jnp.float32)
                out = term if out is None else out + term
        if last:
            gp_sum[...] = out
        else:
            gp_code[z], gp_step[z] = encode(out)
            for item in gp_copies(k, z, place(my_z, z), device):
                item.start()

    if n_z > 1:
        second(1, True, False)
        if n_z <= 4:
            for k in range(2, n_z):
                second(k, False, False)
        else:
            def step(k, carry):
                second(k, False, False)
                return carry
            lax.fori_loop(2, n_z, step, 0)
    second(0, n_z == 1, True)

    def gs_start(k):
        q, device = plane(k)
        gs_code[q], gs_step[q] = encode(gs_acc[q])
        for item in gs_copies(k, q, device):
            item.start()

    each(n_p, gs_start)

    kept = (
        pltpu.make_async_copy(gs_acc.at[my_q], gs_own, local.at[0]),
        pltpu.make_async_copy(gp_sum, gp_own, local.at[1]),
    )
    for item in kept:
        item.start()

    def sent_plane(k):
        q, device = plane(k)
        s_copy(k, q, device).wait_send()
        i_copy(k, q, device).wait_send()
        rs_copy(k, q, device).wait_send()
        for item in gs_copies(k, q, device):
            item.wait()

    def sent_column(k):
        z, device = column(k)
        p_copy(k, z, device).wait_send()
        cs_copy(k, z, device).wait_send()
        for item in gp_copies(k, z, k - 1, device):
            item.wait()

    each(n_p, sent_plane)
    each(n_z, sent_column)
    for item in kept:
        item.wait()


def finish(gs_own, gp_own, gs_got, gp_got, gs_step, gp_step, gs_ref, gp_ref):
    def total(own, codes, steps):
        value = own[...]
        for k in range(codes.shape[0]):
            value += codes[k].astype(jnp.int32).astype(jnp.float32) * steps[k]
        return value

    gs_ref[...] = total(gs_own, gs_got, gs_step)
    gp_ref[...] = total(gp_own, gp_got, gp_step).T


def solution(mesh):
    ranks = mesh.shape["dp"]
    n_p = 1 << (int(math.log2(ranks)) // 2)
    n_z = ranks // n_p

    def shards(spectra, partners, positive):
        rows, embed = spectra.shape
        f32, bf16, i32, i16 = jnp.float32, jnp.bfloat16, jnp.int32, jnp.int16
        vmem, dma = pltpu.VMEM, pltpu.SemaphoreType.DMA
        elements = n_p * n_z * rows * rows
        shapes = [
            ((n_p, rows, embed), bf16),
            ((n_p, embed, rows), bf16),
            ((n_z, rows, embed), bf16),
            ((n_p, 1, rows), i32),
            ((n_p, rows, 128), i32),
            ((n_z, n_p, rows, rows), f32),
            ((n_p, rows, 128), f32),
            ((n_z, 1, rows), f32),
            ((n_p, 2, rows), f32),
            ((n_p, n_p, 1, rows), f32),
            ((n_z, n_z, 1, rows), f32),
            ((n_p, rows, embed), f32),
            ((embed, rows), f32),
            ((n_p, rows, embed), i16),
            ((n_z, embed, rows), i16),
            ((n_p, 1, embed), f32),
            ((n_z, 1, rows), f32),
        ]
        outputs = [jax.ShapeDtypeStruct((rows, embed), f32)] * 2
        parts = [
            ((rows, embed), f32),
            ((embed, rows), f32),
            ((n_p - 1, rows, embed), i16),
            ((n_z - 1, embed, rows), i16),
            ((n_p - 1, 1, embed), f32),
            ((n_z - 1, 1, rows), f32),
        ]
        grads = pl.pallas_call(
            functools.partial(kernel, n_p, n_z),
            out_shape=[jax.ShapeDtypeStruct(shape, kind) for shape, kind in parts],
            in_specs=[pl.BlockSpec(memory_space=pltpu.HBM)] * 3,
            out_specs=[pl.BlockSpec(memory_space=pl.ANY)] * len(parts),
            scratch_shapes=[vmem(shape, kind) for shape, kind in shapes]
            + [dma((n_p,))] * 4 + [dma((n_z,))] * 2
            + [dma((n_p,))] * 2 + [dma((n_z,))] * 2 + [dma((n_p,))] * 2 + [dma((n_z,))] * 2
            + [dma((n_p,))] * 2 + [dma((n_z,))] * 2 + [dma((3,))],
            compiler_params=pltpu.CompilerParams(
                collective_id=0, has_side_effects=True, vmem_limit_bytes=VMEM_BYTES
            ),
            cost_estimate=pl.CostEstimate(
                flops=6 * elements * embed, transcendentals=4 * elements,
                bytes_accessed=8 * rows * embed * (n_p + n_z),
            ),
        )(spectra, partners, positive.reshape(1, rows))
        return pl.pallas_call(
            finish,
            out_shape=outputs,
            in_specs=[pl.BlockSpec(memory_space=pltpu.VMEM)] * len(parts),
            out_specs=[pl.BlockSpec(memory_space=pltpu.VMEM)] * 2,
            compiler_params=pltpu.CompilerParams(vmem_limit_bytes=VMEM_BYTES),
        )(*grads)

    placed = (P(("grp", "dp"), None), P(("grp", "dp"), None), P(("grp", "dp")))
    return jax.shard_map(
        shards,
        mesh=mesh,
        in_specs=placed,
        out_specs=(P(("grp", "dp"), None), P(("grp", "dp"), None)),
        check_vma=False,
    )
```
